32 devices in a mesh: groups: 2 (over y), expert: 4 (over z), dp: 2 (over x), tensor: 2 (over core).
Axes of the slice: x: 2, y: 2, z: 4, core: 2. Of those that a mesh axis runs over, the one named last changes fastest.
Arguments:
- hidden: bfloat16 [32, 2, 4, 80, 768], P(('groups', 'expert'), 'dp', None, None, 'tensor'), parts along dimension 0, may hold values from -6 to 6
- frozen_a: bfloat16 [16, 768, 64], P('expert', 'tensor'), may hold values from -0.21875 to 0.21875
- trained_b: bfloat16 [16, 64, 4096], P('expert', None, 'tensor'), may hold values from -0.75 to 0.75
- routes: int32 [2048, 8], P(('groups', 'expert', 'dp')), parts along dimension 0, may hold values from 0 to 15, all different within a row; in each aligned block of 128 rows (0 to 127, 128 to 255, ...) at most 80 rows name the same one
- gate_weights: float32 [2048, 8], P(('groups', 'expert', 'dp')), parts along dimension 0, may hold values from 0.05 to 0.5
- cotangent: bfloat16 [2048, 4096], P(('groups', 'expert', 'dp'), 'tensor'), parts along dimension 0, may hold values from -6 to 6
Outputs:
- adapter_out: bfloat16 [2048, 4096], P(('groups', 'expert', 'dp'), 'tensor'), parts along dimension 0
- adapter_grad: float32 [32, 64, 4096], P(('groups', 'expert'), 'dp', 'tensor'), parts along dimension 0
- hidden_grad: bfloat16 [32, 2, 4, 80, 768], P(('groups', 'expert'), 'dp', None, None, 'tensor'), parts along dimension 0
The draws below stay inside these ranges and needn't reach their ends.
There are 2 independent parts, one for each index of `groups`. The reference program is written for one: setup_inputs(seed, part) draws one part's arguments, and reference() takes and returns one part's arrays. A program takes and returns all parts, laid end to end along the dimension named above; an argument that names none is the same for every part. Nothing has to cross between parts.
Inputs may be any that keep to these rules, and one draw needn't show every extreme that they name: `routes`: in each aligned block of 128 rows (the rows of one device), no expert is named by more than 80 rows, a bound that some block reaches. Each row names 8 different experts.
All inputs are finite; a program needn't handle non-finite values.
Results may differ from the reference program's by a relative error of at most 0.0057.
Values may be sent and summed in bfloat16 or wider, within the bound.
A program may use at most 128 MiB of HBM per device.

```python
import math
import jax
import jax.numpy as jnp
import numpy as np
from jax import lax

D = 4096
FF = 768
RANK = 64
TOP = 8
TOK_DEV = 128
EXPERTS = 16
TOKENS = 1024
CAP = 80
N_EXPERT = 4
N_DP = 2


def levels(stream_key, extent, pieces, smallest, top_value):
    gain, own = 1.0, jax.random.fold_in(stream_key, 6)
    for dim, shards_of in pieces:
        heights = jnp.exp(jax.random.uniform(jax.random.fold_in(own, dim), (shards_of,), jnp.float32, smallest / len(pieces), top_value / len(pieces)))
        gain = gain * jnp.repeat(heights, extent[dim] // shards_of).reshape([-1 if axis == dim else 1 for axis in range(len(extent))])
    return gain


def shared_out(rng, own, number, rows, amount, top, limit, slope):
    sequence = jax.random.permutation(rng, amount)
    heavy_load, ordinary = shares(amount, rows * top, limit, slope, True), shares(amount, rows * top, limit, slope, False)
    places = jnp.arange(amount)

    def named(tallies, rotation):
        used = int((tallies > 0).sum())
        fixed = max(1, used // 4)
        passed = fixed + (places - fixed + rotation * (used - fixed)) % max(1, amount - fixed)
        return jnp.zeros((amount,), jnp.int32).at[sequence[jnp.where(places < fixed, places, passed)]].set(jnp.asarray(tallies, jnp.int32))

    tallies = jnp.where(number % 4 == 0, named(heavy_load, number // 4), named(ordinary, number - number // 4 - 1))
    mixed = jax.random.permutation(jax.random.fold_in(own, 3), amount)
    donor, sink = mixed[0:amount // 2 * 2:2], mixed[1:amount // 2 * 2:2]
    room = jnp.minimum(tallies[donor] - 1, limit - tallies[sink]) // 2
    room = jnp.where((donor == sequence[0]) | (sink == sequence[0]) | (tallies[sink] == 0), 0, jnp.maximum(room, 0))
    passed = jax.random.randint(jax.random.fold_in(own, 4), (amount // 2,), 0, 1 << 20) % (room + 1)
    tallies = tallies.at[donor].add(-passed).at[sink].add(passed)
    labels = jnp.searchsorted(jnp.cumsum(tallies), jnp.arange(rows * top), side="right").astype(jnp.int32)
    listing = labels.reshape(top, rows).T
    listing = listing[jax.random.permutation(jax.random.fold_in(own, 1), rows)]
    rotation = jax.random.randint(jax.random.fold_in(own, 2), (rows, 1), 0, top)
    return jnp.take_along_axis(listing, (jnp.arange(top)[None, :] + rotation) % top, axis=1)


def shares(count, total, most, skew, full):
    portions = [(1 << 20) // math.isqrt(grade ** skew) + 1 for grade in range(1, count + 1)]
    largest = most if full else min(most, max(-(-total // count), total * portions[0] // sum(portions)))
    least = 1 if total - largest >= count - 1 else 0
    counts, spare = [largest] + [least] * (count - 1), total - largest - least * (count - 1)
    while spare > 0:
        movable = [i for i in range(1, count) if counts[i] < largest] or [i for i in range(1, count) if counts[i] < most]
        mass, left = sum([portions[i] for i in movable]), spare
        for i in movable:
            more = min(most - counts[i], max(1, left * portions[i] // mass), spare)
            counts[i] = counts[i] + more
            spare = spare - more
    return np.array(counts)


def gaussian(stream_key, shape, spread, most, shards=(), held_as=jnp.bfloat16):
    drawn = spread * jax.random.normal(stream_key, shape, jnp.float32)
    if shards:
        drawn = drawn * levels(stream_key, shape, shards, -0.22, 0.18)
    return jnp.clip(drawn, -most, most).astype(held_as)


def setup_inputs(seed: int = 0, part: int = 0) -> dict:
    splits = jax.random.split(jax.random.key(seed), 7)
    part_keys = jax.random.split(jax.random.fold_in(splits[6], part), 7)
    hidden = gaussian(part_keys[0], (EXPERTS, N_DP, N_EXPERT, CAP, FF), 1.0, 6.0, ((0, 4), (1, 2), (4, 2)))
    frozen_a = gaussian(splits[1], (EXPERTS, FF, RANK), FF ** -0.5, 0.21875, ((0, 4), (1, 2)))
    trained_b = gaussian(splits[2], (EXPERTS, RANK, D), RANK ** -0.5, 0.75, ((0, 4), (2, 2)))
    routes_keys = jax.random.split(jax.random.fold_in(part_keys[3], 1), TOKENS // TOK_DEV)
    routes_turns = jax.random.permutation(jax.random.fold_in(part_keys[3], 3), TOKENS // TOK_DEV)
    routes = jax.vmap(lambda own, number: shared_out(jax.random.fold_in(part_keys[3], 2), own, number, TOK_DEV, EXPERTS, TOP, CAP, 2))(routes_keys, routes_turns).reshape((TOKENS, TOP))
    gate_weights = jnp.clip(jnp.exp(math.log(0.5) - 2.3025851 * jax.random.uniform(part_keys[4], (TOKENS, TOP), jnp.float32) ** levels(part_keys[4], (TOKENS, TOP), ((0, 8),), -0.2, 0.2)), 0.05, 0.5)
    cotangent = gaussian(part_keys[5], (TOKENS, D), 1.0, 6.0, ((0, 8), (1, 2)))
    return {"hidden": hidden, "frozen_a": frozen_a, "trained_b": trained_b, "routes": routes, "gate_weights": gate_weights, "cotangent": cotangent}


def route_slots(routes):
    grouped = routes.reshape(-1, TOK_DEV, TOP)
    experts = jnp.arange(EXPERTS, dtype=jnp.int32)
    hit_count = jnp.sum((grouped[:, :, :, None] == experts).astype(jnp.int32), axis=2).astype(jnp.int32)
    before = (jnp.cumsum(hit_count, axis=1) - hit_count).astype(jnp.int32)
    return jnp.take_along_axis(before, grouped, axis=2).reshape(-1, TOP).astype(jnp.int32)


def reference(hidden, frozen_a, trained_b, routes, gate_weights, cotangent):
    blocks = N_EXPERT * N_DP
    slot_rows = blocks * CAP
    slot_place = route_slots(routes)
    stacked = hidden.transpose(0, 2, 1, 3, 4).reshape(EXPERTS, slot_rows, FF)
    block_index = (jnp.arange(TOKENS, dtype=jnp.int32) // TOK_DEV).astype(jnp.int32)
    cot_wide = cotangent.astype(jnp.float32)

    def per_expert(running, inputs):
        expert, hidden_rows, frozen_rows, trained_rows = inputs
        matches = routes == expert
        weight = jnp.sum(jnp.where(matches, gate_weights, jnp.float32(0.0)), axis=1)
        offset = jnp.sum(jnp.where(matches, slot_place, 0), axis=1).astype(jnp.int32)
        row_index = (block_index * CAP + offset).astype(jnp.int32)
        routed = jnp.any(matches, axis=1)
        lowered = jnp.dot(hidden_rows, frozen_rows, preferred_element_type=jnp.float32).astype(jnp.bfloat16)
        slot_out = jnp.dot(lowered, trained_rows, preferred_element_type=jnp.float32).astype(jnp.bfloat16)
        running = running + weight[:, None] * slot_out[row_index].astype(jnp.float32)
        scaled = (weight[:, None] * cot_wide).astype(jnp.bfloat16)
        target = jnp.where(routed, row_index, slot_rows).astype(jnp.int32)
        slot_grad = jnp.zeros((slot_rows + 1, D), jnp.bfloat16).at[target].set(scaled)[:slot_rows]
        grad_rows = jnp.dot(lowered.T, slot_grad, preferred_element_type=jnp.float32)
        projected = jnp.dot(slot_grad, trained_rows.T, preferred_element_type=jnp.float32).astype(jnp.bfloat16)
        grad_hidden = jnp.dot(projected, frozen_rows.T, preferred_element_type=jnp.float32).astype(jnp.bfloat16)
        return running, (grad_rows, grad_hidden)

    start = jnp.zeros((TOKENS, D), jnp.float32)
    experts = jnp.arange(EXPERTS, dtype=jnp.int32)
    running, outputs = lax.scan(per_expert, start, (experts, stacked, frozen_a, trained_b))
    adapter_grad, grad_stack = outputs
    adapter_out = running.astype(jnp.bfloat16)
    hidden_grad = grad_stack.reshape(EXPERTS, N_EXPERT, N_DP, CAP, FF).transpose(0, 2, 1, 3, 4)
    return adapter_out, adapter_grad, hidden_grad
```

```python
import jax
import jax.numpy as jnp
from jax import lax
from jax.sharding import PartitionSpec as P


def token_tables(routes, gate_weights, experts_all):
    rows = routes.shape[0]
    ids = jnp.arange(experts_all, dtype=jnp.int32)
    match = routes.T[:, None, :] == ids[None, :, None]
    gates = jnp.sum(jnp.where(match, gate_weights.T[:, None, :], 0.0), axis=0)
    hits = jnp.any(match, axis=0)
    upper = jnp.triu(jnp.ones((rows, rows), jnp.bfloat16), 1)
    before = jnp.dot(hits.astype(jnp.bfloat16), upper, preferred_element_type=jnp.float32)
    return jnp.stack([jnp.where(hits, before, -1.0), gates])


def local(hidden, frozen_a, trained_b, routes, gate_weights, cotangent):
    f32, bf16 = jnp.float32, jnp.bfloat16
    n_local, _, rank = frozen_a.shape
    blocks = lax.axis_size("expert")
    capacity = hidden.shape[3]
    rows = routes.shape[0]
    tables = token_tables(routes, gate_weights, n_local * blocks)
    tables = lax.all_gather(tables, "expert", axis=0)
    all_cot = lax.all_gather(cotangent, "expert", axis=0)
    tables = lax.dynamic_slice_in_dim(tables, lax.axis_index("expert") * n_local, n_local, 2)
    places, gates = tables[:, 0], tables[:, 1]
    pick = (places[..., None] == jnp.arange(capacity, dtype=f32)).astype(bf16)
    part = jnp.einsum("xscf,xfr->sxcr", hidden[:, 0], frozen_a, preferred_element_type=f32)
    lowered = lax.psum(part, "tensor").astype(bf16)
    low_tok = jnp.einsum("sxtc,sxcr->sxtr", pick, lowered, preferred_element_type=f32)
    low_tok = (low_tok * gates[..., None]).astype(bf16)
    low_tok = low_tok.transpose(0, 2, 1, 3).reshape(blocks, rows, n_local * rank)
    up = trained_b.reshape(n_local * rank, -1)
    out_part = jnp.einsum("str,rd->std", low_tok, up, preferred_element_type=f32).astype(bf16)
    got = lax.all_to_all(out_part, "expert", split_axis=0, concat_axis=0, tiled=True)
    adapter_out = jnp.sum(got.astype(f32), axis=0).astype(bf16)
    back = jnp.einsum("std,rd->str", all_cot, up, preferred_element_type=f32)
    back = lax.psum(back, "tensor").reshape(blocks, rows, n_local, rank)
    back = (back.transpose(0, 2, 1, 3) * gates[..., None]).astype(bf16)
    projected = jnp.einsum("sxtc,sxtr->sxcr", pick, back, preferred_element_type=f32).astype(bf16)
    hidden_grad = jnp.einsum(
        "sxcr,xfr->xscf", projected, frozen_a, preferred_element_type=f32
    ).astype(bf16)
    grad = jnp.einsum("str,std->rd", low_tok, all_cot, preferred_element_type=f32)
    grad = grad.reshape(n_local, rank, -1)
    adapter_grad = lax.psum_scatter(grad, "dp", scatter_dimension=1, tiled=True)
    return adapter_out, adapter_grad, hidden_grad[:, None]


def solution(mesh):
    in_specs = (
        P(("groups", "expert"), "dp", None, None, "tensor"),
        P("expert", "tensor", None),
        P("expert", None, "tensor"),
        P(("groups", "expert", "dp"), None),
        P(("groups", "expert", "dp"), None),
        P(("groups", "expert", "dp"), "tensor"),
    )
    out_specs = (
        P(("groups", "expert", "dp"), "tensor"),
        P(("groups", "expert"), "dp", "tensor"),
        P(("groups", "expert"), "dp", None, None, "tensor"),
    )
    return jax.shard_map(local, mesh=mesh, in_specs=in_specs, out_specs=out_specs, check_vma=False)
```

```python
import functools

import jax
import jax.numpy as jnp
from jax import lax
from jax.experimental import pallas as pl
from jax.experimental.pallas import tpu as pltpu
from jax.sharding import PartitionSpec as P

F32, BF16 = jnp.float32, jnp.bfloat16
MESH = pl.DeviceIdType.MESH
PARTS = 4


def nt_dot(a, b):
    return lax.dot_general(a, b, (((1,), (1,)), ((), ())), preferred_element_type=F32)


def token_tables(routes, gate_weights, experts_all, n_local):
    rows = routes.shape[0]
    ids = jnp.arange(experts_all, dtype=jnp.int32)
    match = routes.T[:, None, :] == ids[None, :, None]
    gates = jnp.sum(jnp.where(match, gate_weights.T[:, None, :], 0.0), axis=0)
    hits = jnp.any(match, axis=0)
    upper = jnp.triu(jnp.ones((rows, rows), BF16), 1)
    before = jnp.dot(hits.astype(BF16), upper, preferred_element_type=F32)
    places = jnp.where(hits, before, -1.0).reshape(-1, n_local, rows)
    return jnp.concatenate([places, gates.reshape(-1, n_local, rows)], axis=1)


def kernel(
    dims, hidden, frozen, up, tables, cot, out, grad, hgrad,
    cot_buf, right_sum, left_sum, tab_buf, low_mine, low_other, pick, low_tr, low_tok,
    back_mine, back_other, grad_out_buf, grad_in_buf,
    tab_send, tab_recv, pair_send, pair_recv,
    fwd_r_send, fwd_l_send, fwd_recv, sum_r_send, sum_l_send, sum_r_recv, sum_l_recv,
    dp_send, dp_recv,
):
    n, n_dp, n_local, rank, cap, rows = dims
    width = up.shape[1]
    part = width // PARTS
    share = rank // n_dp
    me, my_dp, core = lax.axis_index("expert"), lax.axis_index("dp"), lax.axis_index("tensor")
    has_right, has_left = me < n - 1, me > 0

    def cols(q):
        return pl.ds(q * part, part)

    def remote(src, dst, send, recv, where):
        return pltpu.make_async_remote_copy(
            src_ref=src, dst_ref=dst, send_sem=send, recv_sem=recv,
            device_id=where, device_id_type=MESH,
        )

    def fwd_right(q, b):
        block = cot_buf.at[q, b]
        return remote(block, block, fwd_r_send.at[q, b], fwd_recv.at[q, b], {"expert": me + 1})

    def fwd_left(q, b):
        block = cot_buf.at[q, b]
        return remote(block, block, fwd_l_send.at[q, b], fwd_recv.at[q, b], {"expert": me - 1})

    def sum_right(q, j):
        block = right_sum.at[q, j]
        return remote(block, block, sum_r_send.at[q, j], sum_r_recv.at[q, j], {"expert": me + 1})

    def sum_left(q, j):
        block = left_sum.at[q, j]
        return remote(block, block, sum_l_send.at[q, j], sum_l_recv.at[q, j], {"expert": me - 1})

    def tab_copy(k):
        j = lax.rem(me + k, n)
        return remote(tables.at[j], tab_buf.at[me], tab_send.at[k], tab_recv.at[me], {"expert": j})

    def dp_copy(q, d):
        return remote(
            grad_out_buf.at[q, d], grad_in_buf.at[q, my_dp],
            dp_send.at[q, d], dp_recv.at[q, my_dp], {"dp": d},
        )

    def dp_arrival(q, d):
        return remote(
            grad_out_buf.at[q, d], grad_in_buf.at[q, d],
            dp_send.at[q, d], dp_recv.at[q, d], {"dp": d},
        )

    barrier = pltpu.get_barrier_semaphore()
    for k in range(1, n):
        pl.semaphore_signal(
            barrier, inc=1, device_id={"expert": lax.rem(me + k, n)}, device_id_type=MESH
        )
    for k in range(1, n_dp):
        pl.semaphore_signal(
            barrier, inc=1, device_id={"dp": lax.rem(my_dp + k, n_dp)}, device_id_type=MESH
        )
    pl.semaphore_signal(barrier, inc=1, device_id={"tensor": 1 - core}, device_id_type=MESH)
    for q in range(PARTS):
        cot_buf[q, me] = cot[:, q * part : (q + 1) * part]
    tab_buf[me] = tables[me]
    pl.semaphore_wait(barrier, n + n_dp - 1)

    for k in range(1, n):
        tab_copy(k).start()
    for q in range(PARTS):
        @pl.when(has_right)
        def _():
            fwd_right(q, me).start()

        @pl.when(has_left)
        def _():
            fwd_left(q, me).start()

    for x in range(n_local):
        low_mine[x * rank : (x + 1) * rank, :] = lax.dot_general(
            frozen[x], hidden[x], (((0,), (1,)), ((), ())), preferred_element_type=F32
        )
    low_copy = remote(
        low_mine, low_other, pair_send.at[0], pair_recv.at[0], {"tensor": 1 - core}
    )
    low_copy.start()

    for k in range(1, n):
        j = lax.rem(me + k, n)
        remote(
            tables.at[j], tab_buf.at[j], tab_send.at[k], tab_recv.at[j], {"expert": j}
        ).wait_recv()
    slots = lax.broadcasted_iota(jnp.int32, (n * cap, rows), 0).astype(F32)
    for b in range(n):
        tab = tab_buf[b]
        for x in range(n_local):
            want = jnp.where(tab[x : x + 1] >= 0, tab[x : x + 1] + b * cap, -1.0)
            pick[x, :, b * rows : (b + 1) * rows] = jnp.where(slots == want, 1.0, 0.0).astype(BF16)
    low_copy.wait_recv()
    for x in range(n_local):
        span = slice(x * rank, (x + 1) * rank)
        low = (low_mine[span, :] + low_other[span, :]).astype(BF16)
        for b in range(n):
            there = slice(b * rows, (b + 1) * rows)
            chosen = jnp.dot(low, pick[x, :, there], preferred_element_type=F32)
            gated = chosen * tab_buf[b, n_local + x : n_local + x + 1, :]
            low_tr[span, there] = gated
    for b in range(n):
        low_tok[b] = low_tr[:, b * rows : (b + 1) * rows].T.astype(BF16)

    def term(q, j):
        return jnp.dot(low_tok[j], up[:, cols(q)], preferred_element_type=F32)

    def finish_out(q):
        total = term(q, me)
        out_cols = cols(q)

        @pl.when(has_left)
        def _():
            sum_right(q, me).wait_recv()

        @pl.when(jnp.logical_not(has_left))
        def _():
            right_sum[q, me] = jnp.zeros((rows, part), BF16)

        @pl.when(has_right)
        def _():
            sum_left(q, me).wait_recv()

        @pl.when(jnp.logical_not(has_right))
        def _():
            left_sum[q, me] = jnp.zeros((rows, part), BF16)

        total = total + right_sum[q, me].astype(F32) + left_sum[q, me].astype(F32)
        out[:, out_cols] = total.astype(BF16)

    def finish_grad(q):
        for k in range(1, n_dp):
            d = lax.rem(my_dp + k, n_dp)
            dp_arrival(q, d).wait_recv()
            grad[:, cols(q)] += grad_in_buf[q, d].astype(F32)

    for q in range(PARTS):

        def slot(u, carry, q=q):
            from_left = u <= me
            from_right = u <= n - 1 - me
            left_block, right_block = jnp.maximum(me - u, 0), jnp.minimum(me + u, n - 1)

            @pl.when(from_left)
            def _():
                fwd_right(q, left_block).wait_recv()

                @pl.when(has_right)
                def _():
                    fwd_right(q, left_block).start()

            @pl.when(from_right)
            def _():
                fwd_left(q, right_block).wait_recv()

                @pl.when(has_left)
                def _():
                    fwd_left(q, right_block).start()

            @pl.when(jnp.logical_and(u > me, has_right))
            def _():
                j = n + me - u
                mine = term(q, j)

                @pl.when(has_left)
                def _():
                    sum_right(q, j).wait_recv()
                    right_sum[q, j] = (mine + right_sum[q, j].astype(F32)).astype(BF16)

                @pl.when(jnp.logical_not(has_left))
                def _():
                    right_sum[q, j] = mine.astype(BF16)

                sum_right(q, j).start()

            @pl.when(jnp.logical_and(u > n - 1 - me, has_left))
            def _():
                j = u - n + me
                mine = term(q, j)

                @pl.when(has_right)
                def _():
                    sum_left(q, j).wait_recv()
                    left_sum[q, j] = (mine + left_sum[q, j].astype(F32)).astype(BF16)

                @pl.when(jnp.logical_not(has_right))
                def _():
                    left_sum[q, j] = mine.astype(BF16)

                sum_left(q, j).start()

            return carry

        lax.fori_loop(1, n, slot, 0)

        cots = cot_buf[q].reshape(n * rows, part)
        back = nt_dot(up[:, cols(q)], cots)
        if q == 0:
            back_mine[...] = back
        else:
            back_mine[...] += back
        if q == PARTS - 1:
            back_copy = remote(
                back_mine, back_other, pair_send.at[1], pair_recv.at[1], {"tensor": 1 - core}
            )
            back_copy.start()
        full = jnp.dot(low_tr[...].astype(BF16), cots, preferred_element_type=F32)
        full = full.reshape(n_local, rank, part)
        for d in range(n_dp):
            piece = full[:, d * share : (d + 1) * share].reshape(n_local * share, part)

            @pl.when(my_dp == d)
            def _():
                grad[:, cols(q)] = piece

            @pl.when(my_dp != d)
            def _():
                grad_out_buf[q, d] = piece.astype(BF16)
                dp_copy(q, d).start()

        if q > 0:
            finish_out(q - 1)
            finish_grad(q - 1)

    finish_out(PARTS - 1)
    back_copy.wait_recv()
    for x in range(n_local):
        span = slice(x * rank, (x + 1) * rank)
        projected = jnp.zeros((n * cap, rank), F32)
        for b in range(n):
            there = slice(b * rows, (b + 1) * rows)
            both = back_mine[span, there] + back_other[span, there]
            both = (both * tab_buf[b, n_local + x : n_local + x + 1, :]).astype(BF16)
            projected = projected + nt_dot(pick[x, :, there], both)
        hgrad[x] = nt_dot(projected.astype(BF16), frozen[x]).astype(BF16)
    finish_grad(PARTS - 1)

    low_copy.wait_send()
    back_copy.wait_send()
    for k in range(1, n):
        tab_copy(k).wait_send()
    for q in range(PARTS):
        for k in range(1, n_dp):
            dp_copy(q, lax.rem(my_dp + k, n_dp)).wait_send()

        def drain(b, carry, q=q):
            @pl.when(jnp.logical_and(b <= me, has_right))
            def _():
                fwd_right(q, b).wait_send()

            @pl.when(jnp.logical_and(b >= me, has_left))
            def _():
                fwd_left(q, b).wait_send()

            @pl.when(b > me)
            def _():
                sum_right(q, b).wait_send()

            @pl.when(b < me)
            def _():
                sum_left(q, b).wait_send()

            return carry

        lax.fori_loop(0, n, drain, 0)


def local(hidden, frozen_a, trained_b, routes, gate_weights, cotangent):
    n_local, half_ff, rank = frozen_a.shape
    n, n_dp = lax.axis_size("expert"), lax.axis_size("dp")
    cap = hidden.shape[3]
    rows, width = cotangent.shape
    share = rank // n_dp
    part = width // PARTS
    ranks = n_local * rank
    tables = token_tables(routes, gate_weights, n_local * n, n_local)
    vmem = pl.BlockSpec(memory_space=pltpu.VMEM)
    dma = pltpu.SemaphoreType.DMA
    grid_sem = dma((PARTS, n))
    out, grad, hgrad = pl.pallas_call(
        functools.partial(kernel, (n, n_dp, n_local, rank, cap, rows)),
        out_shape=(
            jax.ShapeDtypeStruct((rows, width), BF16),
            jax.ShapeDtypeStruct((n_local * share, width), F32),
            jax.ShapeDtypeStruct((n_local, n * cap, half_ff), BF16),
        ),
        in_specs=[vmem] * 5,
        out_specs=(vmem,) * 3,
        scratch_shapes=[
            pltpu.VMEM((PARTS, n, rows, part), BF16),
            pltpu.VMEM((PARTS, n, rows, part), BF16),
            pltpu.VMEM((PARTS, n, rows, part), BF16),
            pltpu.VMEM((n, 2 * n_local, rows), F32),
            pltpu.VMEM((ranks, n * cap), F32),
            pltpu.VMEM((ranks, n * cap), F32),
            pltpu.VMEM((n_local, n * cap, n * rows), BF16),
            pltpu.VMEM((ranks, n * rows), F32),
            pltpu.VMEM((n, rows, ranks), BF16),
            pltpu.VMEM((ranks, n * rows), F32),
            pltpu.VMEM((ranks, n * rows), F32),
            pltpu.VMEM((PARTS, n_dp, n_local * share, part), BF16),
            pltpu.VMEM((PARTS, n_dp, n_local * share, part), BF16),
            dma((n,)), dma((n,)), dma((2,)), dma((2,)),
            grid_sem, grid_sem, grid_sem, grid_sem, grid_sem, grid_sem, grid_sem,
            dma((PARTS, n_dp)), dma((PARTS, n_dp)),
        ],
        compiler_params=pltpu.CompilerParams(
            collective_id=0, has_side_effects=True, vmem_limit_bytes=60 * 1024 * 1024
        ),
        cost_estimate=pl.CostEstimate(
            flops=2 * 6 * n * rows * ranks * width // 2, bytes_accessed=8 << 20, transcendentals=0
        ),
    )(
        hidden.reshape(n_local, n * cap, half_ff),
        frozen_a,
        trained_b.reshape(ranks, width),
        tables,
        cotangent,
    )
    return (
        out,
        grad.reshape(n_local, share, width),
        hgrad.reshape(n_local, 1, n, cap, half_ff),
    )


def solution(mesh):
    in_specs = (
        P(("groups", "expert"), "dp", None, None, "tensor"),
        P("expert", "tensor", None),
        P("expert", None, "tensor"),
        P(("groups", "expert", "dp"), None),
        P(("groups", "expert", "dp"), None),
        P(("groups", "expert", "dp"), "tensor"),
    )
    out_specs = (
        P(("groups", "expert", "dp"), "tensor"),
        P(("groups", "expert"), "dp", "tensor"),
        P(("groups", "expert"), "dp", None, None, "tensor"),
    )
    return jax.shard_map(local, mesh=mesh, in_specs=in_specs, out_specs=out_specs, check_vma=False)
```

```python
import functools

import jax
import jax.numpy as jnp
from jax import lax
from jax.experimental import pallas as pl
from jax.experimental.pallas import tpu as pltpu
from jax.sharding import PartitionSpec as P

F32, BF16 = jnp.float32, jnp.bfloat16
MESH = pl.DeviceIdType.MESH
PARTS = 4


def nt_dot(a, b):
    return lax.dot_general(a, b, (((1,), (1,)), ((), ())), preferred_element_type=F32)


def token_tables(routes, gate_weights, experts_all, n_local):
    rows = routes.shape[0]
    ids = jnp.arange(experts_all, dtype=jnp.int32)
    match = routes.T[:, None, :] == ids[None, :, None]
    gates = jnp.sum(jnp.where(match, gate_weights.T[:, None, :], 0.0), axis=0)
    hits = jnp.any(match, axis=0)
    upper = jnp.triu(jnp.ones((rows, rows), BF16), 1)
    before = jnp.dot(hits.astype(BF16), upper, preferred_element_type=F32)
    places = jnp.where(hits, before, -1.0).reshape(-1, n_local, rows)
    return jnp.concatenate([places, gates.reshape(-1, n_local, rows)], axis=1)


def kernel(
    dims, hidden, frozen, up, tables, cot, out, grad, hgrad,
    cot_buf, right_sum, left_sum, tab_buf, low_mine, low_other, pick, low_tr, low_tok,
    back_mine, back_other, grad_out_buf, grad_in_buf,
    tab_send, tab_recv, pair_send, pair_recv,
    fwd_r_send, fwd_l_send, fwd_recv, sum_r_send, sum_l_send, sum_r_recv, sum_l_recv,
    dp_send, dp_recv,
):
    n, n_dp, n_local, rank, cap, rows = dims
    width = up.shape[1]
    part = width // PARTS
    share = rank // n_dp
    me, my_dp, core = lax.axis_index("expert"), lax.axis_index("dp"), lax.axis_index("tensor")
    has_right, has_left = me < n - 1, me > 0

    def cols(q):
        return pl.ds(pl.multiple_of(q * part, part), part)

    def remote(src, dst, send, recv, where):
        return pltpu.make_async_remote_copy(
            src_ref=src, dst_ref=dst, send_sem=send, recv_sem=recv,
            device_id=where, device_id_type=MESH,
        )

    def fwd_right(q, b):
        block = cot_buf.at[q, b]
        return remote(block, block, fwd_r_send.at[q, b], fwd_recv.at[q, b], {"expert": me + 1})

    def fwd_left(q, b):
        block = cot_buf.at[q, b]
        return remote(block, block, fwd_l_send.at[q, b], fwd_recv.at[q, b], {"expert": me - 1})

    def sum_right(q, j):
        block = right_sum.at[q, j]
        return remote(block, block, sum_r_send.at[q, j], sum_r_recv.at[q, j], {"expert": me + 1})

    def sum_left(q, j):
        block = left_sum.at[q, j]
        return remote(block, block, sum_l_send.at[q, j], sum_l_recv.at[q, j], {"expert": me - 1})

    def tab_copy(k):
        j = lax.rem(me + k, n)
        return remote(tables.at[j], tab_buf.at[me], tab_send.at[k], tab_recv.at[me], {"expert": j})

    def dp_copy(q, d):
        return remote(
            grad_out_buf.at[q, d], grad_in_buf.at[q, my_dp],
            dp_send.at[q, d], dp_recv.at[q, my_dp], {"dp": d},
        )

    def dp_arrival(q, d):
        return remote(
            grad_out_buf.at[q, d], grad_in_buf.at[q, d],
            dp_send.at[q, d], dp_recv.at[q, d], {"dp": d},
        )

    barrier = pltpu.get_barrier_semaphore()
    for k in range(1, n):
        pl.semaphore_signal(
            barrier, inc=1, device_id={"expert": lax.rem(me + k, n)}, device_id_type=MESH
        )
    for k in range(1, n_dp):
        pl.semaphore_signal(
            barrier, inc=1, device_id={"dp": lax.rem(my_dp + k, n_dp)}, device_id_type=MESH
        )
    pl.semaphore_signal(barrier, inc=1, device_id={"tensor": 1 - core}, device_id_type=MESH)
    for q in range(PARTS):
        cot_buf[q, me] = cot[:, q * part : (q + 1) * part]
    tab_buf[me] = tables[me]
    pl.semaphore_wait(barrier, n + n_dp - 1)

    for k in range(1, n):
        tab_copy(k).start()
    for q in range(PARTS):
        @pl.when(has_right)
        def _():
            fwd_right(q, me).start()

        @pl.when(has_left)
        def _():
            fwd_left(q, me).start()

    for x in range(n_local):
        low_mine[x * rank : (x + 1) * rank, :] = nt_dot(frozen[x], hidden[x])
    low_copy = remote(
        low_mine, low_other, pair_send.at[0], pair_recv.at[0], {"tensor": 1 - core}
    )
    low_copy.start()

    for k in range(1, n):
        j = lax.rem(me + k, n)
        remote(
            tables.at[j], tab_buf.at[j], tab_send.at[k], tab_recv.at[j], {"expert": j}
        ).wait_recv()
    slots = lax.broadcasted_iota(jnp.int32, (n * cap, rows), 0).astype(F32)
    for b in range(n):
        tab = tab_buf[b]
        for x in range(n_local):
            want = jnp.where(tab[x : x + 1] >= 0, tab[x : x + 1] + b * cap, -1.0)
            pick[x, :, b * rows : (b + 1) * rows] = jnp.where(slots == want, 1.0, 0.0).astype(BF16)
    low_copy.wait_recv()
    for x in range(n_local):
        span = slice(x * rank, (x + 1) * rank)
        low = (low_mine[span, :] + low_other[span, :]).astype(BF16)
        for b in range(n):
            there = slice(b * rows, (b + 1) * rows)
            chosen = jnp.dot(low, pick[x, :, there], preferred_element_type=F32)
            gated = chosen * tab_buf[b, n_local + x : n_local + x + 1, :]
            low_tr[span, there] = gated
    for b in range(n):
        low_tok[b] = low_tr[:, b * rows : (b + 1) * rows].T.astype(BF16)

    def term(q, j):
        return jnp.dot(low_tok[j], up[:, cols(q)], preferred_element_type=F32)

    def finish_out(q):
        total = term(q, me)
        out_cols = cols(q)

        @pl.when(has_left)
        def _():
            sum_right(q, me).wait_recv()

        @pl.when(jnp.logical_not(has_left))
        def _():
            right_sum[q, me] = jnp.zeros((rows, part), BF16)

        @pl.when(has_right)
        def _():
            sum_left(q, me).wait_recv()

        @pl.when(jnp.logical_not(has_right))
        def _():
            left_sum[q, me] = jnp.zeros((rows, part), BF16)

        total = total + right_sum[q, me].astype(F32) + left_sum[q, me].astype(F32)
        out[:, out_cols] = total.astype(BF16)

    def finish_grad(q):
        for k in range(1, n_dp):
            d = lax.rem(my_dp + k, n_dp)
            dp_arrival(q, d).wait_recv()
            grad[:, cols(q)] += grad_in_buf[q, d].astype(F32)

    def slot(q, u):
        from_left = u <= me
        from_right = u <= n - 1 - me
        left_block, right_block = jnp.maximum(me - u, 0), jnp.minimum(me + u, n - 1)

        @pl.when(from_left)
        def _():
            fwd_right(q, left_block).wait_recv()

            @pl.when(has_right)
            def _():
                fwd_right(q, left_block).start()

        @pl.when(from_right)
        def _():
            fwd_left(q, right_block).wait_recv()

            @pl.when(has_left)
            def _():
                fwd_left(q, right_block).start()

        @pl.when(jnp.logical_and(u > me, has_right))
        def _():
            j = n + me - u
            mine = term(q, j)

            @pl.when(has_left)
            def _():
                sum_right(q, j).wait_recv()
                right_sum[q, j] = (mine + right_sum[q, j].astype(F32)).astype(BF16)

            @pl.when(jnp.logical_not(has_left))
            def _():
                right_sum[q, j] = mine.astype(BF16)

            sum_right(q, j).start()

        @pl.when(jnp.logical_and(u > n - 1 - me, has_left))
        def _():
            j = u - n + me
            mine = term(q, j)

            @pl.when(has_right)
            def _():
                sum_left(q, j).wait_recv()
                left_sum[q, j] = (mine + left_sum[q, j].astype(F32)).astype(BF16)

            @pl.when(jnp.logical_not(has_right))
            def _():
                left_sum[q, j] = mine.astype(BF16)

            sum_left(q, j).start()

    back_copy = remote(
        back_mine, back_other, pair_send.at[1], pair_recv.at[1], {"tensor": 1 - core}
    )

    def complete(q):
        cots = cot_buf[q].reshape(n * rows, part)
        back_mine[...] += nt_dot(up[:, cols(q)], cots)

        @pl.when(q == PARTS - 1)
        def _():
            back_copy.start()

        full = jnp.dot(low_tr[...].astype(BF16), cots, preferred_element_type=F32)
        full = full.reshape(n_local, rank, part)
        for d in range(n_dp):
            piece = full[:, d * share : (d + 1) * share].reshape(n_local * share, part)

            @pl.when(my_dp == d)
            def _():
                grad[:, cols(q)] = piece

            @pl.when(my_dp != d)
            def _():
                grad_out_buf[q, d] = piece.astype(BF16)
                dp_copy(q, d).start()

    back_mine[...] = jnp.zeros_like(back_mine)

    def step(s, carry):
        def one(q, inner):
            slot(q, s - q)
            return inner

        lax.fori_loop(jnp.maximum(0, s - n + 1), jnp.minimum(PARTS, s), one, 0)

        @pl.when(s >= n - 1)
        def _():
            complete(s - n + 1)

        @pl.when(s >= n)
        def _():
            finish_out(s - n)
            finish_grad(s - n)

        return carry

    lax.fori_loop(1, PARTS + n - 1, step, 0)

    finish_out(PARTS - 1)
    back_copy.wait_recv()
    for x in range(n_local):
        span = slice(x * rank, (x + 1) * rank)
        projected = jnp.zeros((n * cap, rank), F32)
        for b in range(n):
            there = slice(b * rows, (b + 1) * rows)
            both = back_mine[span, there] + back_other[span, there]
            both = (both * tab_buf[b, n_local + x : n_local + x + 1, :]).astype(BF16)
            projected = projected + nt_dot(pick[x, :, there], both)
        hgrad[x] = jnp.dot(
            projected.astype(BF16), frozen[x], preferred_element_type=F32
        ).astype(BF16)
    finish_grad(PARTS - 1)

    low_copy.wait_send()
    back_copy.wait_send()
    for k in range(1, n):
        tab_copy(k).wait_send()
    for q in range(PARTS):
        for k in range(1, n_dp):
            dp_copy(q, lax.rem(my_dp + k, n_dp)).wait_send()

        def drain(b, carry, q=q):
            @pl.when(jnp.logical_and(b <= me, has_right))
            def _():
                fwd_right(q, b).wait_send()

            @pl.when(jnp.logical_and(b >= me, has_left))
            def _():
                fwd_left(q, b).wait_send()

            @pl.when(b > me)
            def _():
                sum_right(q, b).wait_send()

            @pl.when(b < me)
            def _():
                sum_left(q, b).wait_send()

            return carry

        lax.fori_loop(0, n, drain, 0)


def local(hidden, frozen_a, trained_b, routes, gate_weights, cotangent):
    n_local, half_ff, rank = frozen_a.shape
    n, n_dp = lax.axis_size("expert"), lax.axis_size("dp")
    cap = hidden.shape[3]
    rows, width = cotangent.shape
    share = rank // n_dp
    part = width // PARTS
    ranks = n_local * rank
    tables = token_tables(routes, gate_weights, n_local * n, n_local)
    vmem = pl.BlockSpec(memory_space=pltpu.VMEM)
    dma = pltpu.SemaphoreType.DMA
    grid_sem = dma((PARTS, n))
    out, grad, hgrad = pl.pallas_call(
        functools.partial(kernel, (n, n_dp, n_local, rank, cap, rows)),
        out_shape=(
            jax.ShapeDtypeStruct((rows, width), BF16),
            jax.ShapeDtypeStruct((n_local * share, width), F32),
            jax.ShapeDtypeStruct((n_local, n * cap, half_ff), BF16),
        ),
        in_specs=[vmem] * 5,
        out_specs=(vmem,) * 3,
        scratch_shapes=[
            pltpu.VMEM((PARTS, n, rows, part), BF16),
            pltpu.VMEM((PARTS, n, rows, part), BF16),
            pltpu.VMEM((PARTS, n, rows, part), BF16),
            pltpu.VMEM((n, 2 * n_local, rows), F32),
            pltpu.VMEM((ranks, n * cap), F32),
            pltpu.VMEM((ranks, n * cap), F32),
            pltpu.VMEM((n_local, n * cap, n * rows), BF16),
            pltpu.VMEM((ranks, n * rows), F32),
            pltpu.VMEM((n, rows, ranks), BF16),
            pltpu.VMEM((ranks, n * rows), F32),
            pltpu.VMEM((ranks, n * rows), F32),
            pltpu.VMEM((PARTS, n_dp, n_local * share, part), BF16),
            pltpu.VMEM((PARTS, n_dp, n_local * share, part), BF16),
            dma((n,)), dma((n,)), dma((2,)), dma((2,)),
            grid_sem, grid_sem, grid_sem, grid_sem, grid_sem, grid_sem, grid_sem,
            dma((PARTS, n_dp)), dma((PARTS, n_dp)),
        ],
        compiler_params=pltpu.CompilerParams(
            collective_id=0, has_side_effects=True, vmem_limit_bytes=60 * 1024 * 1024
        ),
        cost_estimate=pl.CostEstimate(
            flops=2 * 6 * n * rows * ranks * width // 2, bytes_accessed=8 << 20, transcendentals=0
        ),
    )(
        hidden.reshape(n_local, n * cap, half_ff),
        frozen_a.transpose(0, 2, 1),
        trained_b.reshape(ranks, width),
        tables,
        cotangent,
    )
    return (
        out,
        grad.reshape(n_local, share, width),
        hgrad.reshape(n_local, 1, n, cap, half_ff),
    )


def solution(mesh):
    in_specs = (
        P(("groups", "expert"), "dp", None, None, "tensor"),
        P("expert", "tensor", None),
        P("expert", None, "tensor"),
        P(("groups", "expert", "dp"), None),
        P(("groups", "expert", "dp"), None),
        P(("groups", "expert", "dp"), "tensor"),
    )
    out_specs = (
        P(("groups", "expert", "dp"), "tensor"),
        P(("groups", "expert"), "dp", "tensor"),
        P(("groups", "expert"), "dp", None, None, "tensor"),
    )
    return jax.shard_map(local, mesh=mesh, in_specs=in_specs, out_specs=out_specs, check_vma=False)
```

```python
import functools

import jax
import jax.numpy as jnp
from jax import lax
from jax.experimental import pallas as pl
from jax.experimental.pallas import tpu as pltpu
from jax.sharding import PartitionSpec as P

F32, BF16 = jnp.float32, jnp.bfloat16
MESH = pl.DeviceIdType.MESH
PARTS = 4
LAG = 2


def nt_dot(a, b):
    return lax.dot_general(a, b, (((1,), (1,)), ((), ())), preferred_element_type=F32)


def fill_tables(tables, routes, gate_weights, n, n_local):
    rows = routes.shape[1]
    hit_rows, gate_rows = [], []
    for e in range(n * n_local):
        match = routes == e
        hit_rows.append(jnp.sum(jnp.where(match, 1.0, 0.0), axis=0, keepdims=True))
        gate_rows.append(jnp.sum(jnp.where(match, gate_weights, 0.0), axis=0, keepdims=True))
    hits = jnp.concatenate(hit_rows, axis=0)
    earlier = lax.broadcasted_iota(jnp.int32, (rows, rows), 0)
    upper = earlier < lax.broadcasted_iota(jnp.int32, (rows, rows), 1)
    upper = jnp.where(upper, 1.0, 0.0).astype(BF16)
    before = jnp.dot(hits.astype(BF16), upper, preferred_element_type=F32)
    places = jnp.where(hits > 0, before, -1.0)
    for j in range(n):
        tables[j, 0:n_local] = places[j * n_local : (j + 1) * n_local]
        for x in range(n_local):
            tables[j, n_local + x : n_local + x + 1] = gate_rows[j * n_local + x]


def kernel(
    dims, hidden, frozen, up, routes, gate_weights, cot, out, grad, hgrad,
    cot_buf, right_sum, left_sum, tables, tab_buf, low_mine, low_other, pick, low_f32, low_tr, low_tok,
    proj, back_mine, back_other, grad_out_buf, grad_in_buf,
    tab_send, tab_recv, pair_send, pair_recv,
    fwd_r_send, fwd_l_send, fwd_recv, sum_r_send, sum_l_send, sum_r_recv, sum_l_recv,
    dp_send, dp_recv,
):
    n, n_dp, n_local, rank, cap, rows = dims
    width = up.shape[1]
    part = width // PARTS
    share = rank // n_dp
    me, my_dp, core = lax.axis_index("expert"), lax.axis_index("dp"), lax.axis_index("tensor")
    has_right, has_left = me < n - 1, me > 0

    def cols(q):
        return pl.ds(pl.multiple_of(q * part, part), part)

    def remote(src, dst, send, recv, where):
        return pltpu.make_async_remote_copy(
            src_ref=src, dst_ref=dst, send_sem=send, recv_sem=recv,
            device_id=where, device_id_type=MESH,
        )

    def fwd_right(q, b):
        block = cot_buf.at[q, b]
        return remote(block, block, fwd_r_send.at[q, b], fwd_recv.at[q, b], {"expert": me + 1})

    def fwd_left(q, b):
        block = cot_buf.at[q, b]
        return remote(block, block, fwd_l_send.at[q, b], fwd_recv.at[q, b], {"expert": me - 1})

    def sum_right(q, j):
        block = right_sum.at[q, j]
        return remote(block, block, sum_r_send.at[q, j], sum_r_recv.at[q, j], {"expert": me + 1})

    def sum_left(q, j):
        block = left_sum.at[q, j]
        return remote(block, block, sum_l_send.at[q, j], sum_l_recv.at[q, j], {"expert": me - 1})

    def tab_copy(k):
        j = lax.rem(me + k, n)
        return remote(tables.at[j], tab_buf.at[me], tab_send.at[k], tab_recv.at[me], {"expert": j})

    def dp_copy(q, d):
        return remote(
            grad_out_buf.at[q, d], grad_in_buf.at[q, my_dp],
            dp_send.at[q, d], dp_recv.at[q, my_dp], {"dp": d},
        )

    def dp_arrival(q, d):
        return remote(
            grad_out_buf.at[q, d], grad_in_buf.at[q, d],
            dp_send.at[q, d], dp_recv.at[q, d], {"dp": d},
        )

    barrier = pltpu.get_barrier_semaphore()
    for k in range(1, n):
        pl.semaphore_signal(
            barrier, inc=1, device_id={"expert": lax.rem(me + k, n)}, device_id_type=MESH
        )
    for k in range(1, n_dp):
        pl.semaphore_signal(
            barrier, inc=1, device_id={"dp": lax.rem(my_dp + k, n_dp)}, device_id_type=MESH
        )
    pl.semaphore_signal(barrier, inc=1, device_id={"tensor": 1 - core}, device_id_type=MESH)
    for q in range(PARTS):
        cot_buf[q, me] = cot[:, q * part : (q + 1) * part]
    fill_tables(tables, routes[...], gate_weights[...], n, n_local)
    tab_buf[me] = tables[me]
    pl.semaphore_wait(barrier, n + n_dp - 1)

    for k in range(1, n):
        tab_copy(k).start()
    for q in range(PARTS):
        @pl.when(has_right)
        def _():
            fwd_right(q, me).start()

        @pl.when(has_left)
        def _():
            fwd_left(q, me).start()

    def forward(q, u):
        from_left = u <= me
        from_right = u <= n - 1 - me
        left_block, right_block = jnp.maximum(me - u, 0), jnp.minimum(me + u, n - 1)

        @pl.when(from_left)
        def _():
            fwd_right(q, left_block).wait_recv()

            @pl.when(has_right)
            def _():
                fwd_right(q, left_block).start()

        @pl.when(from_right)
        def _():
            fwd_left(q, right_block).wait_recv()

            @pl.when(has_left)
            def _():
                fwd_left(q, right_block).start()

    def wave(work, s):
        def one(q, inner):
            work(q, s - q)
            return inner

        lax.fori_loop(jnp.maximum(0, s - n + 1), jnp.minimum(PARTS, s), one, 0)

    def forward_step(s):
        wave(forward, s)

    for x in range(n_local):
        low_mine[:, x * rank : (x + 1) * rank] = nt_dot(hidden[x], frozen[x])
    low_copy = remote(
        low_mine, low_other, pair_send.at[0], pair_recv.at[0], {"tensor": 1 - core}
    )
    low_copy.start()

    for k in range(1, n):
        j = lax.rem(me + k, n)
        remote(
            tables.at[j], tab_buf.at[j], tab_send.at[k], tab_recv.at[j], {"expert": j}
        ).wait_recv()
    slot_row = lax.broadcasted_iota(jnp.int32, (cap, rows), 0).astype(F32)
    slot_col = lax.broadcasted_iota(jnp.int32, (rows, cap), 1).astype(F32)
    for b in range(n):
        tab = tab_buf[b]
        for x in range(n_local):
            pick[x, b] = jnp.where(slot_row == tab[x : x + 1], 1.0, 0.0).astype(BF16)
    low_copy.wait_recv()
    for b in range(n):
        if b % 2 == 0 and b // 2 < LAG:
            forward_step(b // 2 + 1)
        down = tab_buf[b].T
        there = slice(b * cap, (b + 1) * cap)
        low = (low_mine[there, :] + low_other[there, :]).astype(BF16)
        for x in range(n_local):
            span = slice(x * rank, (x + 1) * rank)
            chosen = jnp.where(slot_col == down[:, x : x + 1], 1.0, 0.0).astype(BF16)
            rows_low = jnp.dot(chosen, low[:, span], preferred_element_type=F32)
            low_f32[:, span] = rows_low * down[:, n_local + x : n_local + x + 1]
        low_tok[b] = low_f32[...].astype(BF16)
        low_tr[:, b * rows : (b + 1) * rows] = low_f32[...].T.astype(BF16)

    def term(q, j):
        return jnp.dot(low_tok[j], up[:, cols(q)], preferred_element_type=F32)

    def finish_out(q):
        total = term(q, me)
        out_cols = cols(q)

        @pl.when(has_left)
        def _():
            sum_right(q, me).wait_recv()

        @pl.when(jnp.logical_not(has_left))
        def _():
            right_sum[q, me] = jnp.zeros((rows, part), BF16)

        @pl.when(has_right)
        def _():
            sum_left(q, me).wait_recv()

        @pl.when(jnp.logical_not(has_right))
        def _():
            left_sum[q, me] = jnp.zeros((rows, part), BF16)

        total = total + right_sum[q, me].astype(F32) + left_sum[q, me].astype(F32)
        out[:, out_cols] = total.astype(BF16)

    def finish_grad(q):
        for k in range(1, n_dp):
            d = lax.rem(my_dp + k, n_dp)
            dp_arrival(q, d).wait_recv()
            grad[:, cols(q)] += grad_in_buf[q, d].astype(F32)

    def add_sums(q, u):
        @pl.when(jnp.logical_and(u > me, has_right))
        def _():
            j = n + me - u
            mine = term(q, j)

            @pl.when(has_left)
            def _():
                sum_right(q, j).wait_recv()
                right_sum[q, j] = (mine + right_sum[q, j].astype(F32)).astype(BF16)

            @pl.when(jnp.logical_not(has_left))
            def _():
                right_sum[q, j] = mine.astype(BF16)

            sum_right(q, j).start()

        @pl.when(jnp.logical_and(u > n - 1 - me, has_left))
        def _():
            j = u - n + me
            mine = term(q, j)

            @pl.when(has_right)
            def _():
                sum_left(q, j).wait_recv()
                left_sum[q, j] = (mine + left_sum[q, j].astype(F32)).astype(BF16)

            @pl.when(jnp.logical_not(has_right))
            def _():
                left_sum[q, j] = mine.astype(BF16)

            sum_left(q, j).start()

    back_copy = remote(
        back_mine, back_other, pair_send.at[1], pair_recv.at[1], {"tensor": 1 - core}
    )

    def complete(q):
        cots = cot_buf[q].reshape(n * rows, part)
        back_mine[...] += nt_dot(up[:, cols(q)], cots)

        @pl.when(q == PARTS - 1)
        def _():
            back_copy.start()

        full = jnp.dot(low_tr[...], cots, preferred_element_type=F32)
        full = full.reshape(n_local, rank, part)
        for d in range(n_dp):
            piece = full[:, d * share : (d + 1) * share].reshape(n_local * share, part)

            @pl.when(my_dp == d)
            def _():
                grad[:, cols(q)] = piece

            @pl.when(my_dp != d)
            def _():
                grad_out_buf[q, d] = piece.astype(BF16)
                dp_copy(q, d).start()

    back_mine[...] = jnp.zeros_like(back_mine)
    last = PARTS + n - 2

    def step(s, carry):
        forward_step(s)
        wave(add_sums, s - LAG)

        @pl.when(s >= n - 1)
        def _():
            complete(s - n + 1)

        @pl.when(s >= n)
        def _():
            finish_grad(s - n)

        @pl.when(s >= n + LAG)
        def _():
            finish_out(s - n - LAG)

        return carry

    lax.fori_loop(LAG + 1, last + 1, step, 0)
    for s in range(last + 1, last + LAG + 1):
        wave(add_sums, s - LAG)
        if s == last + 1:
            back_copy.wait_recv()
            for b in range(n):
                for x in range(n_local):
                    span, there = slice(x * rank, (x + 1) * rank), slice(b * rows, (b + 1) * rows)
                    both = back_mine[span, there] + back_other[span, there]
                    both = (both * tab_buf[b, n_local + x : n_local + x + 1, :]).astype(BF16)
                    proj[b * cap : (b + 1) * cap, span] = nt_dot(pick[x, b], both)
        if s == last + LAG:
            for x in range(n_local):
                hgrad[x] = jnp.dot(
                    proj[:, x * rank : (x + 1) * rank].astype(BF16), frozen[x],
                    preferred_element_type=F32,
                ).astype(BF16)
            finish_grad(PARTS - 1)
        if s - n - LAG >= 0:
            finish_out(s - n - LAG)
    for q in range(max(0, last - n + 1), PARTS):
        finish_out(q)

    low_copy.wait_send()
    back_copy.wait_send()
    for k in range(1, n):
        tab_copy(k).wait_send()
    for q in range(PARTS):
        for k in range(1, n_dp):
            dp_copy(q, lax.rem(my_dp + k, n_dp)).wait_send()

        def drain(b, carry, q=q):
            @pl.when(jnp.logical_and(b <= me, has_right))
            def _():
                fwd_right(q, b).wait_send()

            @pl.when(jnp.logical_and(b >= me, has_left))
            def _():
                fwd_left(q, b).wait_send()

            @pl.when(b > me)
            def _():
                sum_right(q, b).wait_send()

            @pl.when(b < me)
            def _():
                sum_left(q, b).wait_send()

            return carry

        lax.fori_loop(0, n, drain, 0)


def local(hidden, frozen_a, trained_b, routes, gate_weights, cotangent):
    n_local, half_ff, rank = frozen_a.shape
    n, n_dp = lax.axis_size("expert"), lax.axis_size("dp")
    cap = hidden.shape[3]
    rows, width = cotangent.shape
    share = rank // n_dp
    part = width // PARTS
    ranks = n_local * rank
    vmem = pl.BlockSpec(memory_space=pltpu.VMEM)
    dma = pltpu.SemaphoreType.DMA
    grid_sem = dma((PARTS, n))
    out, grad, hgrad = pl.pallas_call(
        functools.partial(kernel, (n, n_dp, n_local, rank, cap, rows)),
        out_shape=(
            jax.ShapeDtypeStruct((rows, width), BF16),
            jax.ShapeDtypeStruct((n_local * share, width), F32),
            jax.ShapeDtypeStruct((n_local, n * cap, half_ff), BF16),
        ),
        in_specs=[vmem] * 6,
        out_specs=(vmem,) * 3,
        scratch_shapes=[
            pltpu.VMEM((PARTS, n, rows, part), BF16),
            pltpu.VMEM((PARTS, n, rows, part), BF16),
            pltpu.VMEM((PARTS, n, rows, part), BF16),
            pltpu.VMEM((n, 2 * n_local, rows), F32),
            pltpu.VMEM((n, 2 * n_local, rows), F32),
            pltpu.VMEM((n * cap, ranks), F32),
            pltpu.VMEM((n * cap, ranks), F32),
            pltpu.VMEM((n_local, n, cap, rows), BF16),
            pltpu.VMEM((rows, ranks), F32),
            pltpu.VMEM((ranks, n * rows), BF16),
            pltpu.VMEM((n, rows, ranks), BF16),
            pltpu.VMEM((n * cap, ranks), F32),
            pltpu.VMEM((ranks, n * rows), F32),
            pltpu.VMEM((ranks, n * rows), F32),
            pltpu.VMEM((PARTS, n_dp, n_local * share, part), BF16),
            pltpu.VMEM((PARTS, n_dp, n_local * share, part), BF16),
            dma((n,)), dma((n,)), dma((2,)), dma((2,)),
            grid_sem, grid_sem, grid_sem, grid_sem, grid_sem, grid_sem, grid_sem,
            dma((PARTS, n_dp)), dma((PARTS, n_dp)),
        ],
        compiler_params=pltpu.CompilerParams(
            collective_id=0, has_side_effects=True, vmem_limit_bytes=60 * 1024 * 1024
        ),
        cost_estimate=pl.CostEstimate(
            flops=2 * 6 * n * rows * ranks * width // 2, bytes_accessed=8 << 20, transcendentals=0
        ),
    )(
        hidden.reshape(n_local, n * cap, half_ff),
        frozen_a.transpose(0, 2, 1),
        trained_b.reshape(ranks, width),
        routes.T,
        gate_weights.T,
        cotangent,
    )
    return (
        out,
        grad.reshape(n_local, share, width),
        hgrad.reshape(n_local, 1, n, cap, half_ff),
    )


def solution(mesh):
    in_specs = (
        P(("groups", "expert"), "dp", None, None, "tensor"),
        P("expert", "tensor", None),
        P("expert", None, "tensor"),
        P(("groups", "expert", "dp"), None),
        P(("groups", "expert", "dp"), None),
        P(("groups", "expert", "dp"), "tensor"),
    )
    out_specs = (
        P(("groups", "expert", "dp"), "tensor"),
        P(("groups", "expert"), "dp", "tensor"),
        P(("groups", "expert"), "dp", None, None, "tensor"),
    )
    return jax.shard_map(local, mesh=mesh, in_specs=in_specs, out_specs=out_specs, check_vma=False)
```

```python
import functools

import jax
import jax.numpy as jnp
from jax import lax
from jax.experimental import pallas as pl
from jax.experimental.pallas import tpu as pltpu
from jax.sharding import PartitionSpec as P

F32, BF16 = jnp.float32, jnp.bfloat16
MESH = pl.DeviceIdType.MESH
PARTS = 2


def nt_dot(a, b):
    return lax.dot_general(a, b, (((1,), (1,)), ((), ())), preferred_element_type=F32)


def fill_tables(tables, routes, gate_weights, n, n_local):
    rows = routes.shape[1]
    hit_rows, gate_rows = [], []
    for e in range(n * n_local):
        match = routes == e
        hit_rows.append(jnp.sum(jnp.where(match, 1.0, 0.0), axis=0, keepdims=True))
        gate_rows.append(jnp.sum(jnp.where(match, gate_weights, 0.0), axis=0, keepdims=True))
    hits = jnp.concatenate(hit_rows, axis=0)
    earlier = lax.broadcasted_iota(jnp.int32, (rows, rows), 0)
    upper = earlier < lax.broadcasted_iota(jnp.int32, (rows, rows), 1)
    upper = jnp.where(upper, 1.0, 0.0).astype(BF16)
    before = jnp.dot(hits.astype(BF16), upper, preferred_element_type=F32)
    places = jnp.where(hits > 0, before, -1.0)
    for j in range(n):
        tables[j, 0:n_local] = places[j * n_local : (j + 1) * n_local]
        for x in range(n_local):
            tables[j, n_local + x : n_local + x + 1] = gate_rows[j * n_local + x]


def kernel(
    dims, hidden, frozen, up, routes, gate_weights, cot, out, grad, hgrad,
    cot_buf, right_sum, left_sum, tables, tab_buf, low_mine, low_other, pick, low_f32, low_tr, low_tok,
    proj, back_mine, back_other, grad_out_buf, grad_in_buf,
    tab_send, tab_recv, pair_send, pair_recv,
    fwd_r_send, fwd_l_send, fwd_recv, sum_r_send, sum_l_send, sum_r_recv, sum_l_recv,
    dp_send, dp_recv,
):
    n, n_dp, n_local, rank, cap, rows = dims
    width = up.shape[1]
    part = width // PARTS
    share = rank // n_dp
    me, my_dp, core = lax.axis_index("expert"), lax.axis_index("dp"), lax.axis_index("tensor")
    has_right, has_left = me < n - 1, me > 0

    def cols(q):
        return pl.ds(pl.multiple_of(q * part, part), part)

    def remote(src, dst, send, recv, where):
        return pltpu.make_async_remote_copy(
            src_ref=src, dst_ref=dst, send_sem=send, recv_sem=recv,
            device_id=where, device_id_type=MESH,
        )

    def fwd_right(q, b):
        block = cot_buf.at[q, b]
        return remote(block, block, fwd_r_send.at[q, b], fwd_recv.at[q, b], {"expert": me + 1})

    def fwd_left(q, b):
        block = cot_buf.at[q, b]
        return remote(block, block, fwd_l_send.at[q, b], fwd_recv.at[q, b], {"expert": me - 1})

    def sum_right(q, j):
        block = right_sum.at[q, j]
        return remote(block, block, sum_r_send.at[q, j], sum_r_recv.at[q, j], {"expert": me + 1})

    def sum_left(q, j):
        block = left_sum.at[q, j]
        return remote(block, block, sum_l_send.at[q, j], sum_l_recv.at[q, j], {"expert": me - 1})

    def tab_copy(k):
        j = lax.rem(me + k, n)
        return remote(tables.at[j], tab_buf.at[me], tab_send.at[k], tab_recv.at[me], {"expert": j})

    def dp_copy(q, d):
        return remote(
            grad_out_buf.at[q, d], grad_in_buf.at[q, my_dp],
            dp_send.at[q, d], dp_recv.at[q, my_dp], {"dp": d},
        )

    def dp_arrival(q, d):
        return remote(
            grad_out_buf.at[q, d], grad_in_buf.at[q, d],
            dp_send.at[q, d], dp_recv.at[q, d], {"dp": d},
        )

    barrier = pltpu.get_barrier_semaphore()
    for k in range(1, n):
        pl.semaphore_signal(
            barrier, inc=1, device_id={"expert": lax.rem(me + k, n)}, device_id_type=MESH
        )
    for k in range(1, n_dp):
        pl.semaphore_signal(
            barrier, inc=1, device_id={"dp": lax.rem(my_dp + k, n_dp)}, device_id_type=MESH
        )
    pl.semaphore_signal(barrier, inc=1, device_id={"tensor": 1 - core}, device_id_type=MESH)
    for q in range(PARTS):
        cot_buf[q, me] = cot[:, q * part : (q + 1) * part]
    fill_tables(tables, routes[...], gate_weights[...], n, n_local)
    tab_buf[me] = tables[me]
    pl.semaphore_wait(barrier, n + n_dp - 1)

    for k in range(1, n):
        tab_copy(k).start()
    for q in range(PARTS):
        @pl.when(has_right)
        def _():
            fwd_right(q, me).start()

        @pl.when(has_left)
        def _():
            fwd_left(q, me).start()

    def forward(q, u):
        from_left = u <= me
        from_right = u <= n - 1 - me
        left_block, right_block = jnp.maximum(me - u, 0), jnp.minimum(me + u, n - 1)

        @pl.when(from_left)
        def _():
            fwd_right(q, left_block).wait_recv()

            @pl.when(has_right)
            def _():
                fwd_right(q, left_block).start()

        @pl.when(from_right)
        def _():
            fwd_left(q, right_block).wait_recv()

            @pl.when(has_left)
            def _():
                fwd_left(q, right_block).start()

    def wave(work, s):
        def one(q, inner):
            work(q, s - q)
            return inner

        lax.fori_loop(jnp.maximum(0, s - n + 1), jnp.minimum(PARTS, s), one, 0)

    def exchange(q, u):
        add_sums(q, u)
        forward(q, u)

    for x in range(n_local):
        low_mine[:, x * rank : (x + 1) * rank] = nt_dot(hidden[x], frozen[x])
    low_copy = remote(
        low_mine, low_other, pair_send.at[0], pair_recv.at[0], {"tensor": 1 - core}
    )
    low_copy.start()

    for k in range(1, n):
        j = lax.rem(me + k, n)
        remote(
            tables.at[j], tab_buf.at[j], tab_send.at[k], tab_recv.at[j], {"expert": j}
        ).wait_recv()
    slot_row = lax.broadcasted_iota(jnp.int32, (cap, rows), 0).astype(F32)
    slot_col = lax.broadcasted_iota(jnp.int32, (rows, cap), 1).astype(F32)
    for b in range(n):
        tab = tab_buf[b]
        for x in range(n_local):
            pick[x, b] = jnp.where(slot_row == tab[x : x + 1], 1.0, 0.0).astype(BF16)
    low_copy.wait_recv()
    for b in range(n):
        down = tab_buf[b].T
        there = slice(b * cap, (b + 1) * cap)
        low = (low_mine[there, :] + low_other[there, :]).astype(BF16)
        for x in range(n_local):
            span = slice(x * rank, (x + 1) * rank)
            chosen = jnp.where(slot_col == down[:, x : x + 1], 1.0, 0.0).astype(BF16)
            rows_low = jnp.dot(chosen, low[:, span], preferred_element_type=F32)
            low_f32[:, span] = rows_low * down[:, n_local + x : n_local + x + 1]
        low_tok[b] = low_f32[...].astype(BF16)
        low_tr[:, b * rows : (b + 1) * rows] = low_f32[...].T.astype(BF16)

    def term(q, j):
        return jnp.dot(low_tok[j], up[:, cols(q)], preferred_element_type=F32)

    def finish_out(q):
        total = term(q, me)
        out_cols = cols(q)

        @pl.when(has_left)
        def _():
            sum_right(q, me).wait_recv()

        @pl.when(jnp.logical_not(has_left))
        def _():
            right_sum[q, me] = jnp.zeros((rows, part), BF16)

        @pl.when(has_right)
        def _():
            sum_left(q, me).wait_recv()

        @pl.when(jnp.logical_not(has_right))
        def _():
            left_sum[q, me] = jnp.zeros((rows, part), BF16)

        total = total + right_sum[q, me].astype(F32) + left_sum[q, me].astype(F32)
        out[:, out_cols] = total.astype(BF16)

    def finish_grad(q):
        for k in range(1, n_dp):
            d = lax.rem(my_dp + k, n_dp)
            dp_arrival(q, d).wait_recv()
            grad[:, cols(q)] += grad_in_buf[q, d].astype(F32)

    def add_sums(q, u):
        @pl.when(jnp.logical_and(u > me, has_right))
        def _():
            j = n + me - u
            mine = term(q, j)

            @pl.when(has_left)
            def _():
                sum_right(q, j).wait_recv()
                right_sum[q, j] = (mine + right_sum[q, j].astype(F32)).astype(BF16)

            @pl.when(jnp.logical_not(has_left))
            def _():
                right_sum[q, j] = mine.astype(BF16)

            sum_right(q, j).start()

        @pl.when(jnp.logical_and(u > n - 1 - me, has_left))
        def _():
            j = u - n + me
            mine = term(q, j)

            @pl.when(has_right)
            def _():
                sum_left(q, j).wait_recv()
                left_sum[q, j] = (mine + left_sum[q, j].astype(F32)).astype(BF16)

            @pl.when(jnp.logical_not(has_right))
            def _():
                left_sum[q, j] = mine.astype(BF16)

            sum_left(q, j).start()

    back_copy = remote(
        back_mine, back_other, pair_send.at[1], pair_recv.at[1], {"tensor": 1 - core}
    )

    def complete(q):
        cots = cot_buf[q].reshape(n * rows, part)
        back_mine[...] += nt_dot(up[:, cols(q)], cots)

        @pl.when(q == PARTS - 1)
        def _():
            back_copy.start()

        full = jnp.dot(low_tr[...], cots, preferred_element_type=F32)
        full = full.reshape(n_local, rank, part)
        for d in range(n_dp):
            piece = full[:, d * share : (d + 1) * share].reshape(n_local * share, part)

            @pl.when(my_dp == d)
            def _():
                grad[:, cols(q)] = piece

            @pl.when(my_dp != d)
            def _():
                grad_out_buf[q, d] = piece.astype(BF16)
                dp_copy(q, d).start()

    back_mine[...] = jnp.zeros_like(back_mine)
    last = PARTS + n - 2

    def step(s, carry):
        wave(exchange, s)

        @pl.when(s >= n - 1)
        def _():
            complete(s - n + 1)

        @pl.when(s >= n)
        def _():
            finish_grad(s - n)
            finish_out(s - n)

        return carry

    lax.fori_loop(1, last + 1, step, 0)
    finish_out(PARTS - 1)
    back_copy.wait_recv()
    for b in range(n):
        for x in range(n_local):
            span, there = slice(x * rank, (x + 1) * rank), slice(b * rows, (b + 1) * rows)
            both = back_mine[span, there] + back_other[span, there]
            both = (both * tab_buf[b, n_local + x : n_local + x + 1, :]).astype(BF16)
            proj[b * cap : (b + 1) * cap, span] = nt_dot(pick[x, b], both)
    for x in range(n_local):
        hgrad[x] = jnp.dot(
            proj[:, x * rank : (x + 1) * rank].astype(BF16), frozen[x],
            preferred_element_type=F32,
        ).astype(BF16)
    finish_grad(PARTS - 1)

    low_copy.wait_send()
    back_copy.wait_send()
    for k in range(1, n):
        tab_copy(k).wait_send()
    for q in range(PARTS):
        for k in range(1, n_dp):
            dp_copy(q, lax.rem(my_dp + k, n_dp)).wait_send()

        def drain(b, carry, q=q):
            @pl.when(jnp.logical_and(b <= me, has_right))
            def _():
                fwd_right(q, b).wait_send()

            @pl.when(jnp.logical_and(b >= me, has_left))
            def _():
                fwd_left(q, b).wait_send()

            @pl.when(b > me)
            def _():
                sum_right(q, b).wait_send()

            @pl.when(b < me)
            def _():
                sum_left(q, b).wait_send()

            return carry

        lax.fori_loop(0, n, drain, 0)


def local(hidden, frozen_a, trained_b, routes, gate_weights, cotangent):
    n_local, half_ff, rank = frozen_a.shape
    n, n_dp = lax.axis_size("expert"), lax.axis_size("dp")
    cap = hidden.shape[3]
    rows, width = cotangent.shape
    share = rank // n_dp
    part = width // PARTS
    ranks = n_local * rank
    vmem = pl.BlockSpec(memory_space=pltpu.VMEM)
    dma = pltpu.SemaphoreType.DMA
    grid_sem = dma((PARTS, n))
    out, grad, hgrad = pl.pallas_call(
        functools.partial(kernel, (n, n_dp, n_local, rank, cap, rows)),
        out_shape=(
            jax.ShapeDtypeStruct((rows, width), BF16),
            jax.ShapeDtypeStruct((n_local * share, width), F32),
            jax.ShapeDtypeStruct((n_local, n * cap, half_ff), BF16),
        ),
        in_specs=[vmem] * 6,
        out_specs=(vmem,) * 3,
        scratch_shapes=[
            pltpu.VMEM((PARTS, n, rows, part), BF16),
            pltpu.VMEM((PARTS, n, rows, part), BF16),
            pltpu.VMEM((PARTS, n, rows, part), BF16),
            pltpu.VMEM((n, 2 * n_local, rows), F32),
            pltpu.VMEM((n, 2 * n_local, rows), F32),
            pltpu.VMEM((n * cap, ranks), F32),
            pltpu.VMEM((n * cap, ranks), F32),
            pltpu.VMEM((n_local, n, cap, rows), BF16),
            pltpu.VMEM((rows, ranks), F32),
            pltpu.VMEM((ranks, n * rows), BF16),
            pltpu.VMEM((n, rows, ranks), BF16),
            pltpu.VMEM((n * cap, ranks), F32),
            pltpu.VMEM((ranks, n * rows), F32),
            pltpu.VMEM((ranks, n * rows), F32),
            pltpu.VMEM((PARTS, n_dp, n_local * share, part), BF16),
            pltpu.VMEM((PARTS, n_dp, n_local * share, part), BF16),
            dma((n,)), dma((n,)), dma((2,)), dma((2,)),
            grid_sem, grid_sem, grid_sem, grid_sem, grid_sem, grid_sem, grid_sem,
            dma((PARTS, n_dp)), dma((PARTS, n_dp)),
        ],
        compiler_params=pltpu.CompilerParams(
            collective_id=0, has_side_effects=True, vmem_limit_bytes=60 * 1024 * 1024
        ),
        cost_estimate=pl.CostEstimate(
            flops=2 * 6 * n * rows * ranks * width // 2, bytes_accessed=8 << 20, transcendentals=0
        ),
    )(
        hidden.reshape(n_local, n * cap, half_ff),
        frozen_a.transpose(0, 2, 1),
        trained_b.reshape(ranks, width),
        routes.T,
        gate_weights.T,
        cotangent,
    )
    return (
        out,
        grad.reshape(n_local, share, width),
        hgrad.reshape(n_local, 1, n, cap, half_ff),
    )


def solution(mesh):
    in_specs = (
        P(("groups", "expert"), "dp", None, None, "tensor"),
        P("expert", "tensor", None),
        P("expert", None, "tensor"),
        P(("groups", "expert", "dp"), None),
        P(("groups", "expert", "dp"), None),
        P(("groups", "expert", "dp"), "tensor"),
    )
    out_specs = (
        P(("groups", "expert", "dp"), "tensor"),
        P(("groups", "expert"), "dp", "tensor"),
        P(("groups", "expert"), "dp", None, None, "tensor"),
    )
    return jax.shard_map(local, mesh=mesh, in_specs=in_specs, out_specs=out_specs, check_vma=False)
```
